32 devices in a mesh: parts: 2 (over y), blk: 4 (over z), row: 2 (over x), sub: 2 (over core).
Axes of the slice: x: 2, y: 2, z: 4, core: 2. Of those that a mesh axis runs over, the one named last changes fastest.
Arguments:
- query_grads: bfloat16 [512, 4, 2048], P('blk', None, 'sub'), may hold values from -6 to 6
- curvature: bfloat16 [4, 2048, 2048], P('blk', ('row', 'sub')), may hold values from -0.125 to 0.125
- train_grads: bfloat16 [5120, 4, 2048], P(('parts', 'row', 'sub'), 'blk'), parts along dimension 0, may hold values from -0.0625 to 0.0625
- query_ids: int32 [1024], P('parts'), parts along dimension 0, may hold values from 0 to 511, each once
- block_map: int32 [4], replicated, may hold values from 0 to 3, each once
- row_ids: int32 [5120], P(('parts', 'row', 'sub')), parts along dimension 0, may hold values from 0 to 639
Outputs:
- scores: float32 [512, 5120], P('blk', ('parts', 'row', 'sub')), parts along dimension 1
The draws below stay inside these ranges and needn't reach their ends.
There are 2 independent parts, one for each index of `parts`. The reference program is written for one: setup_inputs(seed, part) draws one part's arguments, and reference() takes and returns one part's arrays. A program takes and returns all parts, laid end to end along the dimension named above; an argument that names none is the same for every part. Nothing has to cross between parts.
Inputs may be any that keep to these rules, and one draw needn't show every extreme that they name: `query_ids`: each value appears once. `block_map`: each value appears once.
All inputs are finite; a program needn't handle non-finite values.
Results may differ from the reference program's by a relative error of at most 0.0029.
Values may be sent and summed in bfloat16 or wider, within the bound.
A program may use at most 64 MiB of HBM per device.

```python
import jax
import jax.numpy as jnp
from jax import lax

K = 2048
Q = 512
R_DEV = 640
L = 4
R = 2560


def with_ends(values, key, least, largest):
    longest = values.shape.index(max(values.shape))
    spots = []
    for shift in (0, 1):
        where = [jax.random.randint(jax.random.fold_in(key, axis), (), 0, length) for axis, length in enumerate(values.shape)]
        where[longest] = (where[longest] + shift) % values.shape[longest]
        spots.append(tuple(where))
    return values.at[spots[0]].set(least).at[spots[1]].set(largest)


def with_spikes(entries, rng, source, target, shards_of, factor):
    def block_of(position):
        return (jnp.arange(entries.shape[position]) // (entries.shape[position] // shards_of)).reshape((-1,) + (1,) * (entries.ndim - 1 - position))

    one_side = jax.random.permutation(rng, shards_of)[block_of(target)]
    far = (block_of(target) + shards_of // 2) % shards_of
    return jnp.where((block_of(source) == one_side) | (block_of(source) == far), factor * entries, entries)


def shard_levels(key, dims, shards, smallest, largest):
    def one(position, shards_of):
        steps = jax.random.uniform(jax.random.fold_in(jax.random.fold_in(key, 6), position), (shards_of,), jnp.float32, smallest / len(shards), largest / len(shards))
        return jnp.repeat(jnp.exp(steps), dims[position] // shards_of).reshape((-1,) + (1,) * (len(dims) - position - 1))

    gain = one(*shards[0])
    for cut in shards[1:]:
        gain = gain * one(*cut)
    return gain


def bell_draw(own_key, shape, width, bound, split=(), held_as=jnp.bfloat16):
    array = jax.random.normal(own_key, shape, jnp.float32) * width
    if len(split) > 0:
        array = shard_levels(own_key, shape, split, -0.22, 0.18) * array
    return jnp.clip(array, min=-bound, max=bound).astype(held_as)


def noise_with(own_key, dims, spread, most, shards, heavy, kind=jnp.bfloat16):
    drawn = spread * jax.random.normal(own_key, dims, jnp.float32)
    if shards:
        drawn = drawn * shard_levels(own_key, dims, shards, -0.22, 0.18)
    return jnp.clip(with_spikes(drawn, jax.random.fold_in(own_key, 3), *heavy), -most, most).astype(kind)


def setup_inputs(seed: int = 0, part: int = 0) -> dict:
    splits = jax.random.split(jax.random.key(seed), 7)
    part_keys = jax.random.split(jax.random.fold_in(splits[6], part), 7)
    return {
        "query_grads": noise_with(splits[0], (Q, L, K), 1.0, 6.0, ((0, 4), (2, 2)), (1, 0, 4, 2.0)),
        "curvature": bell_draw(splits[1], (L, K, K), K ** -0.5, 0.125, ((0, 4), (1, 4))),
        "train_grads": bell_draw(part_keys[2], (R, L, K), (L * K) ** -0.5, 0.0625, ((0, 4), (1, 4))),
        "query_ids": jax.random.permutation(part_keys[3], Q).astype(jnp.int32),
        "block_map": jax.random.permutation(splits[4], L).astype(jnp.int32),
        "row_ids": with_ends(jax.random.randint(part_keys[5], (R,), 0, R_DEV), jax.random.fold_in(part_keys[5], 1), 0, R_DEV - 1).astype(jnp.int32),
    }


def reference(query_grads, curvature, train_grads, query_ids, block_map, row_ids):
    grouped = jnp.take(query_grads, block_map, axis=1)

    def one_slot(pair):
        block, grads = pair
        return jnp.dot(grads, block.T, preferred_element_type=jnp.float32).astype(jnp.bfloat16)

    precond = lax.map(one_slot, (curvature, jnp.swapaxes(grouped, 0, 1)))
    precond = jnp.swapaxes(precond, 0, 1)
    total_rows = row_ids.shape[0]
    starts = (jnp.arange(total_rows, dtype=jnp.int32) // R_DEV) * R_DEV
    chosen = jnp.take(train_grads, (starts + row_ids).astype(jnp.int32), axis=0)
    flat_q = precond.reshape(precond.shape[0], -1)
    flat_r = chosen.reshape(chosen.shape[0], -1)
    total = jnp.dot(flat_q, flat_r.T, preferred_element_type=jnp.float32)
    scores = jnp.zeros(total.shape, jnp.float32).at[query_ids].set(total)
    return scores
```

```python
import functools

import jax
import jax.numpy as jnp
from jax import lax
from jax.experimental import pallas as pl
from jax.experimental.pallas import tpu as pltpu
from jax.sharding import PartitionSpec as P

MESH = pl.DeviceIdType.MESH
F32 = jnp.float32
BF16 = jnp.bfloat16
NT = (((1,), (1,)), ((), ()))
TN = (((0,), (0,)), ((), ()))


def aligned(index, size):
    return pl.ds(pl.multiple_of(index * size, size), size)


def kernel(
    nb, nx, names,
    block_map, query_ids, row_ids, q_hbm, curv_hbm, train_hbm, out_ref,
    q_ref, curv, train, chosen, stage, grouped, precond, mine, sent, arrived,
    load_sem, z_send, z_recv, a_send, a_recv, c_send, c_recv, e_send, e_recv,
):
    p, b, r, s = (lax.axis_index(name) for name in ("parts", "blk", "row", "sub"))
    rows = q_ref.shape[0]
    half = q_ref.shape[1] // nb
    piece = half // (2 * nx)
    own_cols = curv.shape[0]
    part_cols = own_cols // 2

    def at(parts=None, blk=None, row=None, sub=None):
        return (
            p if parts is None else parts,
            b if blk is None else blk,
            r if row is None else row,
            s if sub is None else sub,
        )

    loads = [
        pltpu.make_async_copy(q_hbm, q_ref, load_sem.at[0]),
        pltpu.make_async_copy(train_hbm, train, load_sem.at[1]),
        pltpu.make_async_copy(curv_hbm, curv, load_sem.at[2]),
    ]
    for load in loads:
        load.start()

    other = 1 - s
    mate = 1 - p
    peers = [lax.rem(r + o, nx) for o in range(nx)]
    origins = [lax.rem(r + nx - o, nx) for o in range(nx)]
    sources = [lax.rem(b + d, nb) for d in range(nb)]

    barrier = pltpu.get_barrier_semaphore()
    everyone = [at(blk=sources[d]) for d in range(1, nb)]
    everyone += [at(row=peers[o]) for o in range(1, nx)]
    everyone += [at(parts=mate), at(sub=other)]
    for device in everyone:
        pl.semaphore_signal(barrier, inc=1, device_id=device, device_id_type=MESH)

    loads[0].wait()
    for d in range(nb):
        target = lax.rem(b + nb - d, nb)

        def add(block, total, slot=block_map[target]):
            weight = jnp.where(slot == block, 1.0, 0.0)
            values = q_ref[:, aligned(block * 2 * nx + p * nx + r, piece)]
            return total + weight * values.astype(F32)

        zeros = jnp.zeros((rows, piece), F32)
        block = lax.fori_loop(0, nb, add, zeros, unroll=nb <= 8).astype(BF16)
        if d:
            stage[d] = block
        else:
            grouped[aligned(b, rows), aligned(s * 2 * nx + p * nx + r, piece)] = block
    pl.semaphore_wait(barrier, len(everyone))

    started = []

    def remote(ref_from, ref_to, send, recv, device):
        return pltpu.make_async_remote_copy(
            src_ref=ref_from, dst_ref=ref_to, send_sem=send, recv_sem=recv,
            device_id=device, device_id_type=MESH,
        )

    def go(*args):
        copy = remote(*args)
        copy.start()
        started.append(copy)

    def arrive(ref, send, recv):
        remote(ref, ref, send, recv, at(sub=other)).wait_recv()

    def spot(d, parts, row):
        return grouped.at[aligned(sources[d], rows), aligned(s * 2 * nx + parts * nx + row, piece)]

    def half_spot(d, sub):
        return grouped.at[aligned(sources[d], rows), aligned(sub, half)]

    def p_spot(d, row, sub):
        return precond.at[aligned(sources[d], rows), aligned(row * 2 + sub, own_cols)]

    def p_half(d, row, sub, parts):
        return precond.at[
            aligned(sources[d], rows), aligned((row * 2 + sub) * 2 + parts, part_cols)
        ]

    for d in range(1, nb):
        go(stage.at[d], spot(0, p, r), z_send.at[d], z_recv.at[d], at(blk=lax.rem(b + nb - d, nb)))

    def spread(d):
        if d:
            arrive(spot(d, p, r), z_send.at[d], z_recv.at[d])
        for o in range(1, nx):
            go(spot(d, p, r), spot(d, p, r), a_send.at[d, o], a_recv.at[d, o], at(row=peers[o]))
        go(spot(d, p, r), spot(d, p, r), a_send.at[d, nx], a_recv.at[d, nx], at(parts=mate))

    def second(d):
        for o in range(1, nx):
            arrive(spot(d, p, origins[o]), a_send.at[d, o], a_recv.at[d, o])
            if d % 2 == 0:
                place = spot(d, p, origins[o])
                go(place, place, a_send.at[d, nx + o], a_recv.at[d, nx + o], at(parts=mate))
        arrive(spot(d, mate, r), a_send.at[d, nx], a_recv.at[d, nx])
        if d % 2 == 1:
            place = spot(d, mate, r)
            for o in range(1, nx):
                go(place, place, a_send.at[d, nx + o], a_recv.at[d, nx + o], at(row=peers[o]))

    def across(d):
        for o in range(1, nx):
            arrive(spot(d, mate, origins[o]), a_send.at[d, nx + o], a_recv.at[d, nx + o])
        place = half_spot(d, s)
        go(place, place, a_send.at[d, 2 * nx], a_recv.at[d, 2 * nx], at(sub=other))

    def apply(d):
        arrive(half_spot(d, other), a_send.at[d, 2 * nx], a_recv.at[d, 2 * nx])
        result = lax.dot_general(
            grouped[aligned(sources[d], rows), :], curv[...], NT, preferred_element_type=F32
        )
        precond[aligned(sources[d], rows), aligned(r * 2 + s, own_cols)] = result.astype(BF16)
        place = p_half(d, r, s, p)
        for o in range(1, nx):
            go(place, place, c_send.at[d, o], c_recv.at[d, o], at(row=peers[o]))
        place = p_spot(d, r, s)
        go(place, place, c_send.at[d, 0], c_recv.at[d, 0], at(sub=other))

    def forward(d):
        for o in range(1, nx):
            place = p_half(d, origins[o], s, p)
            arrive(place, c_send.at[d, o], c_recv.at[d, o])
            go(place, place, c_send.at[d, nx + o], c_recv.at[d, nx + o], at(parts=mate))

    def share(d):
        for o in range(1, nx):
            arrive(p_half(d, origins[o], s, mate), c_send.at[d, nx + o], c_recv.at[d, nx + o])
            place = p_spot(d, origins[o], s)
            go(place, place, c_send.at[d, 2 * nx + o], c_recv.at[d, 2 * nx + o], at(sub=other))

    def finish(d):
        arrive(p_spot(d, r, other), c_send.at[d, 0], c_recv.at[d, 0])
        for o in range(1, nx):
            arrive(p_spot(d, origins[o], other), c_send.at[d, 2 * nx + o], c_recv.at[d, 2 * nx + o])

    def choose():
        loads[1].wait()
        count = train.shape[0]
        pick = (lax.broadcasted_iota(jnp.int32, (count, count), 0) == row_ids[...])
        pick = jnp.where(pick, 1.0, 0.0).astype(BF16)
        width = 512

        @pl.loop(0, train.shape[1] // width)
        def _(step):
            chosen[:, aligned(step, width)] = lax.dot_general(
                pick, train[:, aligned(step, width)], TN, preferred_element_type=F32
            ).astype(BF16)

    steps = [spread, second, across, apply, forward, share, finish]
    for t in range(nb + len(steps) - 1):
        for lag, step in enumerate(steps):
            if 0 <= t - lag < nb:
                step(t - lag)
        if t == 0:
            choose()
            loads[2].wait()

    def score(target):
        outs = lax.broadcasted_iota(jnp.int32, (rows, precond.shape[0]), 0) + target * rows
        pick = jnp.where(outs == query_ids[...], 1.0, 0.0).astype(BF16)
        ordered = jnp.dot(pick, precond[...], preferred_element_type=F32).astype(BF16)
        return lax.dot_general(ordered, chosen[...], NT, preferred_element_type=F32)

    def exchange(e):
        target = lax.rem(b + e, nb)
        return remote(sent.at[e], arrived.at[e], e_send.at[e], e_recv.at[e], at(blk=target))

    @pl.loop(1, nb)
    def _(e):
        sent[e] = score(lax.rem(b + e, nb)).astype(BF16)
        exchange(e).start()

    mine[...] = score(b)
    for copy in started:
        copy.wait_send()

    @pl.loop(1, nb)
    def _(e):
        exchange(e).wait()
        mine[...] += arrived[e].astype(F32)

    out_ref[...] = mine[...]


def per_device(nb, nx, names, query_grads, curvature, train_grads, query_ids, block_map, row_ids):
    rows, blocks, half = query_grads.shape
    queries = query_ids.shape[0]
    features = curvature.shape[2]
    count = train_grads.shape[0]
    smem = pl.BlockSpec(memory_space=pltpu.SMEM)
    vmem = pl.BlockSpec(memory_space=pltpu.VMEM)
    hbm = pl.BlockSpec(memory_space=pl.ANY)
    dma = pltpu.SemaphoreType.DMA
    return pl.pallas_call(
        functools.partial(kernel, nb, nx, names),
        out_shape=jax.ShapeDtypeStruct((rows, count), F32),
        in_specs=[smem, vmem, vmem, hbm, hbm, hbm],
        out_specs=vmem,
        scratch_shapes=[
            pltpu.VMEM((rows, blocks * half), BF16),
            pltpu.VMEM(curvature.shape[1:], BF16),
            pltpu.VMEM((count, features), BF16),
            pltpu.VMEM((count, features), BF16),
            pltpu.VMEM((nb, rows, half // (2 * nx)), BF16),
            pltpu.VMEM((queries, features), BF16),
            pltpu.VMEM((queries, features), BF16),
            pltpu.VMEM((rows, count), F32),
            pltpu.VMEM((nb, rows, count), BF16),
            pltpu.VMEM((nb, rows, count), BF16),
            dma((3,)),
            dma((nb,)),
            dma((nb,)),
            dma((nb, 2 * nx + 1)),
            dma((nb, 2 * nx + 1)),
            dma((nb, 3 * nx)),
            dma((nb, 3 * nx)),
            dma((nb,)),
            dma((nb,)),
        ],
        compiler_params=pltpu.CompilerParams(
            collective_id=0, has_side_effects=True, vmem_limit_bytes=63 * 2**20
        ),
        cost_estimate=pl.CostEstimate(
            flops=2 * queries * features * (curvature.shape[1] + count),
            bytes_accessed=8 * 2**20,
            transcendentals=0,
        ),
    )(
        block_map,
        query_ids.reshape(1, queries),
        row_ids.reshape(1, count),
        query_grads.reshape(rows, blocks * half),
        curvature.reshape(curvature.shape[1:]),
        train_grads.reshape(count, features),
    )


def solution(mesh):
    placed = (
        P("blk", None, "sub"),
        P("blk", ("row", "sub"), None),
        P(("parts", "row", "sub"), "blk", None),
        P("parts"),
        P(),
        P(("parts", "row", "sub")),
    )
    return jax.shard_map(
        functools.partial(per_device, mesh.shape["blk"], mesh.shape["row"], mesh.axis_names),
        mesh=mesh,
        in_specs=placed,
        out_specs=P("blk", ("parts", "row", "sub")),
        check_vma=False,
    )
```

```python
import functools

import jax
import jax.numpy as jnp
from jax import lax
from jax.experimental import pallas as pl
from jax.experimental.pallas import tpu as pltpu
from jax.sharding import PartitionSpec as P

MESH = pl.DeviceIdType.MESH
F32 = jnp.float32
BF16 = jnp.bfloat16
NT = (((1,), (1,)), ((), ()))


def aligned(index, size):
    return pl.ds(pl.multiple_of(index * size, size), size)


def kernel(
    nb, nx, names,
    block_map, query_ids, row_ids, q_hbm, curv_hbm, train_hbm, out_ref,
    q_ref, curv, train, chosen, row_pick, stage, grouped, precond, mine, sent, arrived,
    load_sem, z_send, z_recv, a_send, a_recv, c_send, c_recv, e_send, e_recv,
):
    p, b, r, s = (lax.axis_index(name) for name in ("parts", "blk", "row", "sub"))
    rows = q_ref.shape[0]
    piece = q_ref.shape[1] // nb
    half = 2 * nx * piece
    own_cols = curv.shape[0]

    def at(parts=None, blk=None, row=None, sub=None):
        return (
            p if parts is None else parts,
            b if blk is None else blk,
            r if row is None else row,
            s if sub is None else sub,
        )

    loads = [
        pltpu.make_async_copy(q_hbm, q_ref, load_sem.at[0]),
        pltpu.make_async_copy(train_hbm, train, load_sem.at[1]),
        pltpu.make_async_copy(curv_hbm, curv, load_sem.at[2]),
    ]
    for load in loads:
        load.start()

    other = 1 - s
    mate = 1 - p
    peers = [lax.rem(r + o, nx) for o in range(nx)]
    origins = [lax.rem(r + nx - o, nx) for o in range(nx)]
    sources = [lax.rem(b + d, nb) for d in range(nb)]

    barrier = pltpu.get_barrier_semaphore()
    everyone = [at(blk=sources[d]) for d in range(1, nb)]
    everyone += [at(row=peers[o]) for o in range(1, nx)]
    everyone += [at(parts=mate), at(sub=other)]
    for device in everyone:
        pl.semaphore_signal(barrier, inc=1, device_id=device, device_id_type=MESH)

    loads[0].wait()
    for d in range(nb):
        target = lax.rem(b + nb - d, nb)

        def add(block, total, slot=block_map[target]):
            weight = jnp.where(slot == block, 1.0, 0.0)
            return total + weight * q_ref[:, aligned(block, piece)].astype(F32)

        zeros = jnp.zeros((rows, piece), F32)
        block = lax.fori_loop(0, nb, add, zeros, unroll=nb <= 8).astype(BF16)
        if d:
            stage[d] = block
        else:
            grouped[aligned(b, rows), aligned(s * 2 * nx + p * nx + r, piece)] = block
    pl.semaphore_wait(barrier, len(everyone))

    started = []

    def remote(ref_from, ref_to, send, recv, device):
        return pltpu.make_async_remote_copy(
            src_ref=ref_from, dst_ref=ref_to, send_sem=send, recv_sem=recv,
            device_id=device, device_id_type=MESH,
        )

    def go(*args):
        copy = remote(*args)
        copy.start()
        started.append(copy)

    def arrive(ref, send, recv):
        remote(ref, ref, send, recv, at(sub=other)).wait_recv()

    def spot(d, parts, row):
        return grouped.at[aligned(sources[d], rows), aligned(s * 2 * nx + parts * nx + row, piece)]

    def half_spot(d, sub):
        return grouped.at[aligned(sources[d], rows), aligned(sub, half)]

    def p_spot(e, row, sub):
        return precond.at[aligned(sources[e], rows), aligned(row * 2 + sub, own_cols)]

    for d in range(1, nb):
        go(stage.at[d], spot(0, p, r), z_send.at[d], z_recv.at[d], at(blk=lax.rem(b + nb - d, nb)))

    def spread(d):
        if d:
            arrive(spot(d, p, r), z_send.at[d], z_recv.at[d])
        for o in range(1, nx):
            go(spot(d, p, r), spot(d, p, r), a_send.at[d, o], a_recv.at[d, o], at(row=peers[o]))
        go(spot(d, p, r), spot(d, p, r), a_send.at[d, nx], a_recv.at[d, nx], at(parts=mate))

    def second(d):
        for o in range(1, nx):
            arrive(spot(d, p, origins[o]), a_send.at[d, o], a_recv.at[d, o])
            if d % 2 == 0:
                place = spot(d, p, origins[o])
                go(place, place, a_send.at[d, nx + o], a_recv.at[d, nx + o], at(parts=mate))
        arrive(spot(d, mate, r), a_send.at[d, nx], a_recv.at[d, nx])
        if d % 2 == 1:
            place = spot(d, mate, r)
            for o in range(1, nx):
                go(place, place, a_send.at[d, nx + o], a_recv.at[d, nx + o], at(row=peers[o]))

    def across(d):
        for o in range(1, nx):
            arrive(spot(d, mate, origins[o]), a_send.at[d, nx + o], a_recv.at[d, nx + o])
        place = half_spot(d, s)
        go(place, place, a_send.at[d, 2 * nx], a_recv.at[d, 2 * nx], at(sub=other))

    def settle(d):
        arrive(half_spot(d, other), a_send.at[d, 2 * nx], a_recv.at[d, 2 * nx])

    count = train.shape[0]
    width = train.shape[1] // nb

    def choose(d):
        if d == 0:
            loads[1].wait()
            pick = lax.broadcasted_iota(jnp.int32, (count, count), 0) == row_ids[...].reshape(1, count)
            row_pick[...] = jnp.where(pick, 1.0, 0.0).astype(BF16).T
        if width % 128 == 0 or d == 0:
            cols = pl.ds(d * width, width) if width % 128 == 0 else pl.ds(0, train.shape[1])
            chosen[:, cols] = jnp.dot(
                row_pick[...], train[:, cols], preferred_element_type=F32
            ).astype(BF16)

    def pipeline(steps, count):
        for t in range(count + max(lag for lag, _ in steps)):
            for lag, step in steps:
                if 0 <= t - lag < count:
                    step(t - lag)

    pipeline([(0, spread), (1, second), (0, choose), (2, across), (3, settle)], nb)
    loads[2].wait()

    def apply(e):
        outs = lax.broadcasted_iota(jnp.int32, (rows, grouped.shape[0]), 0) + sources[e] * rows
        pick = jnp.where(outs == query_ids[...], 1.0, 0.0).astype(BF16)
        ordered = jnp.dot(pick, grouped[...], preferred_element_type=F32).astype(BF16)
        result = lax.dot_general(ordered, curv[...], NT, preferred_element_type=F32)
        precond[aligned(sources[e], rows), aligned(r * 2 + s, own_cols)] = result.astype(BF16)
        place = p_spot(e, r, s)
        for o in range(1, nx):
            go(place, place, c_send.at[e, o], c_recv.at[e, o], at(row=peers[o]))
        go(place, place, c_send.at[e, 0], c_recv.at[e, 0], at(sub=other))

    def share(e):
        for o in range(1, nx):
            place = p_spot(e, origins[o], s)
            arrive(place, c_send.at[e, o], c_recv.at[e, o])
            go(place, place, c_send.at[e, nx + o], c_recv.at[e, nx + o], at(sub=other))

    def score(e):
        arrive(p_spot(e, r, other), c_send.at[e, 0], c_recv.at[e, 0])
        for o in range(1, nx):
            arrive(p_spot(e, origins[o], other), c_send.at[e, nx + o], c_recv.at[e, nx + o])
        result = lax.dot_general(
            precond[aligned(sources[e], rows), :], chosen[...], NT, preferred_element_type=F32
        )
        if e:
            sent[e] = result.astype(BF16)
            exchange(e).start()
        else:
            mine[...] = result

    def exchange(e):
        target = lax.rem(b + e, nb)
        return remote(sent.at[e], arrived.at[e], e_send.at[e], e_recv.at[e], at(blk=target))

    def turn(step):
        return lambda t: step((t + 1) % nb)

    pipeline([(0, turn(apply)), (2, turn(score)), (1, turn(share))], nb)
    for copy in started:
        copy.wait_send()

    @pl.loop(1, nb)
    def _(e):
        exchange(e).wait()
        mine[...] += arrived[e].astype(F32)

    out_ref[...] = mine[...]


def per_device(nb, nx, names, query_grads, curvature, train_grads, query_ids, block_map, row_ids):
    rows, blocks, half = query_grads.shape
    queries = query_ids.shape[0]
    features = curvature.shape[2]
    count = train_grads.shape[0]
    piece = half // (2 * nx)
    spot = lax.axis_index("parts") * nx + lax.axis_index("row")
    part = lax.dynamic_slice_in_dim(query_grads, spot * piece, piece, axis=2)
    smem = pl.BlockSpec(memory_space=pltpu.SMEM)
    vmem = pl.BlockSpec(memory_space=pltpu.VMEM)
    hbm = pl.BlockSpec(memory_space=pl.ANY)
    dma = pltpu.SemaphoreType.DMA
    return pl.pallas_call(
        functools.partial(kernel, nb, nx, names),
        out_shape=jax.ShapeDtypeStruct((rows, count), F32),
        in_specs=[smem, vmem, vmem, hbm, hbm, hbm],
        out_specs=vmem,
        scratch_shapes=[
            pltpu.VMEM((rows, blocks * piece), BF16),
            pltpu.VMEM(curvature.shape[1:], BF16),
            pltpu.VMEM((count, features), BF16),
            pltpu.VMEM((count, features), BF16),
            pltpu.VMEM((count, count), BF16),
            pltpu.VMEM((nb, rows, piece), BF16),
            pltpu.VMEM((queries, features), BF16),
            pltpu.VMEM((queries, features), BF16),
            pltpu.VMEM((rows, count), F32),
            pltpu.VMEM((nb, rows, count), BF16),
            pltpu.VMEM((nb, rows, count), BF16),
            dma((3,)),
            dma((nb,)),
            dma((nb,)),
            dma((nb, 2 * nx + 1)),
            dma((nb, 2 * nx + 1)),
            dma((nb, 2 * nx)),
            dma((nb, 2 * nx)),
            dma((nb,)),
            dma((nb,)),
        ],
        compiler_params=pltpu.CompilerParams(
            collective_id=0, has_side_effects=True, vmem_limit_bytes=62 * 2**20
        ),
        cost_estimate=pl.CostEstimate(
            flops=2 * queries * features * (curvature.shape[1] + count),
            bytes_accessed=8 * 2**20,
            transcendentals=0,
        ),
    )(
        block_map,
        query_ids.reshape(1, queries),
        row_ids,
        part.reshape(rows, blocks * piece),
        curvature.reshape(curvature.shape[1:]),
        train_grads.reshape(count, features),
    )


def solution(mesh):
    placed = (
        P("blk", None, "sub"),
        P("blk", ("row", "sub"), None),
        P(("parts", "row", "sub"), "blk", None),
        P("parts"),
        P(),
        P(("parts", "row", "sub")),
    )
    return jax.shard_map(
        functools.partial(per_device, mesh.shape["blk"], mesh.shape["row"], mesh.axis_names),
        mesh=mesh,
        in_specs=placed,
        out_specs=P("blk", ("parts", "row", "sub")),
        check_vma=False,
    )
```

```python
import functools

import jax
import jax.numpy as jnp
from jax import lax
from jax.experimental import pallas as pl
from jax.experimental.pallas import tpu as pltpu
from jax.sharding import PartitionSpec as P

MESH = pl.DeviceIdType.MESH
F32 = jnp.float32
BF16 = jnp.bfloat16
NT = (((1,), (1,)), ((), ()))


def aligned(index, size):
    return pl.ds(pl.multiple_of(index * size, size), size)


def kernel(
    nb, nx, names,
    block_map, query_ids, row_ids, q_hbm, curv_hbm, train_hbm, out_ref,
    q_ref, curv, train, chosen, row_pick, stage, grouped, precond, mine, sent, arrived,
    load_sem, z_send, z_recv, a_send, a_recv, c_send, c_recv, e_send, e_recv,
):
    p, b, r, s = (lax.axis_index(name) for name in ("parts", "blk", "row", "sub"))
    rows = q_ref.shape[0]
    piece = q_ref.shape[1] // nb
    half = 2 * nx * piece
    own_cols = curv.shape[0]

    def at(parts=None, blk=None, row=None, sub=None):
        return (
            p if parts is None else parts,
            b if blk is None else blk,
            r if row is None else row,
            s if sub is None else sub,
        )

    loads = [
        pltpu.make_async_copy(q_hbm, q_ref, load_sem.at[0]),
        pltpu.make_async_copy(train_hbm, train, load_sem.at[1]),
        pltpu.make_async_copy(curv_hbm, curv, load_sem.at[2]),
    ]
    for load in loads:
        load.start()

    other = 1 - s
    mate = 1 - p
    peers = [lax.rem(r + o, nx) for o in range(nx)]
    origins = [lax.rem(r + nx - o, nx) for o in range(nx)]
    sources = [lax.rem(b + d, nb) for d in range(nb)]

    barrier = pltpu.get_barrier_semaphore()
    everyone = [at(blk=sources[d]) for d in range(1, nb)]
    everyone += [at(row=peers[o]) for o in range(1, nx)]
    everyone += [at(parts=mate), at(sub=other)]
    for device in everyone:
        pl.semaphore_signal(barrier, inc=1, device_id=device, device_id_type=MESH)

    loads[0].wait()
    for d in range(nb):
        target = lax.rem(b + nb - d, nb)

        def add(block, total, slot=block_map[target]):
            weight = jnp.where(slot == block, 1.0, 0.0)
            return total + weight * q_ref[:, aligned(block, piece)].astype(F32)

        zeros = jnp.zeros((rows, piece), F32)
        block = lax.fori_loop(0, nb, add, zeros, unroll=nb <= 8).astype(BF16)
        if d:
            stage[d] = block
        else:
            grouped[aligned(b, rows), aligned(s * 2 * nx + p * nx + r, piece)] = block
    pl.semaphore_wait(barrier, len(everyone))

    started = []

    def remote(ref_from, ref_to, send, recv, device):
        return pltpu.make_async_remote_copy(
            src_ref=ref_from, dst_ref=ref_to, send_sem=send, recv_sem=recv,
            device_id=device, device_id_type=MESH,
        )

    def go(*args):
        copy = remote(*args)
        copy.start()
        started.append(copy)

    def arrive(ref, send, recv):
        remote(ref, ref, send, recv, at(sub=other)).wait_recv()

    def spot(d, parts, row):
        return grouped.at[aligned(sources[d], rows), aligned(s * 2 * nx + parts * nx + row, piece)]

    def half_spot(d, sub):
        return grouped.at[aligned(sources[d], rows), aligned(sub, half)]

    def p_spot(e, row, sub):
        return precond.at[aligned(sources[e], rows), aligned(row * 2 + sub, own_cols)]

    for d in range(1, nb):
        go(stage.at[d], spot(0, p, r), z_send.at[d], z_recv.at[d], at(blk=lax.rem(b + nb - d, nb)))

    def spread(d):
        if d:
            arrive(spot(d, p, r), z_send.at[d], z_recv.at[d])
        for o in range(1, nx):
            go(spot(d, p, r), spot(d, p, r), a_send.at[d, o], a_recv.at[d, o], at(row=peers[o]))
        go(spot(d, p, r), spot(d, p, r), a_send.at[d, nx], a_recv.at[d, nx], at(parts=mate))

    def second(d):
        for o in range(1, nx):
            arrive(spot(d, p, origins[o]), a_send.at[d, o], a_recv.at[d, o])
            if d % 2 == 0:
                place = spot(d, p, origins[o])
                go(place, place, a_send.at[d, nx + o], a_recv.at[d, nx + o], at(parts=mate))
        arrive(spot(d, mate, r), a_send.at[d, nx], a_recv.at[d, nx])
        if d % 2 == 1:
            place = spot(d, mate, r)
            for o in range(1, nx):
                go(place, place, a_send.at[d, nx + o], a_recv.at[d, nx + o], at(row=peers[o]))

    def across(d):
        for o in range(1, nx):
            arrive(spot(d, mate, origins[o]), a_send.at[d, nx + o], a_recv.at[d, nx + o])
        place = half_spot(d, s)
        go(place, place, a_send.at[d, 2 * nx], a_recv.at[d, 2 * nx], at(sub=other))

    def settle(d):
        arrive(half_spot(d, other), a_send.at[d, 2 * nx], a_recv.at[d, 2 * nx])

    count = train.shape[0]
    width = train.shape[1] // nb

    def choose(d):
        if d == 0:
            loads[1].wait()
            pick = lax.broadcasted_iota(jnp.int32, (count, count), 0) == row_ids[...].reshape(1, count)
            row_pick[...] = jnp.where(pick, 1.0, 0.0).astype(BF16).T
        if width % 128 == 0 or d == 0:
            cols = pl.ds(d * width, width) if width % 128 == 0 else pl.ds(0, train.shape[1])
            chosen[:, cols] = jnp.dot(
                row_pick[...], train[:, cols], preferred_element_type=F32
            ).astype(BF16)

    def pipeline(steps, count):
        for t in range(count + max(lag for lag, _ in steps)):
            for lag, step in steps:
                if 0 <= t - lag < count:
                    step(t - lag)

    pipeline([(0, spread), (1, second), (0, choose), (2, across), (3, settle)], nb)
    loads[2].wait()

    def apply(e):
        outs = lax.broadcasted_iota(jnp.int32, (rows, grouped.shape[0]), 0) + sources[e] * rows
        pick = jnp.where(outs == query_ids[...], 1.0, 0.0).astype(BF16)
        ordered = jnp.dot(pick, grouped[...], preferred_element_type=F32).astype(BF16)
        result = lax.dot_general(ordered, curv[...], NT, preferred_element_type=F32)
        precond[aligned(sources[e], rows), aligned(r * 2 + s, own_cols)] = result.astype(BF16)
        place = p_spot(e, r, s)
        for o in range(1, nx):
            go(place, place, c_send.at[e, o], c_recv.at[e, o], at(row=peers[o]))
        go(place, place, c_send.at[e, 0], c_recv.at[e, 0], at(sub=other))

    def share(e):
        for o in range(1, nx):
            place = p_spot(e, origins[o], s)
            arrive(place, c_send.at[e, o], c_recv.at[e, o])
            go(place, place, c_send.at[e, nx + o], c_recv.at[e, nx + o], at(sub=other))

    def score(e):
        arrive(p_spot(e, r, other), c_send.at[e, 0], c_recv.at[e, 0])
        for o in range(1, nx):
            arrive(p_spot(e, origins[o], other), c_send.at[e, nx + o], c_recv.at[e, nx + o])
        result = lax.dot_general(
            precond[aligned(sources[e], rows), :], chosen[...], NT, preferred_element_type=F32
        )
        if e:
            sent[e] = result.astype(BF16)
            exchange(e).start()
        else:
            mine[...] = result

    def exchange(e):
        target = lax.rem(b + e, nb)
        return remote(sent.at[e], arrived.at[e], e_send.at[e], e_recv.at[e], at(blk=target))

    order = sorted(range(1, nb), key=lambda e: abs(2 * e - nb)) + [0]

    def turn(step):
        return lambda t: step(order[t])

    pipeline([(0, turn(apply)), (2, turn(score)), (1, turn(share))], nb)
    for copy in started:
        copy.wait_send()

    @pl.loop(1, nb)
    def _(e):
        exchange(e).wait()
        mine[...] += arrived[e].astype(F32)

    out_ref[...] = mine[...]


def per_device(nb, nx, names, query_grads, curvature, train_grads, query_ids, block_map, row_ids):
    rows, blocks, half = query_grads.shape
    queries = query_ids.shape[0]
    features = curvature.shape[2]
    count = train_grads.shape[0]
    piece = half // (2 * nx)
    spot = lax.axis_index("parts") * nx + lax.axis_index("row")
    part = lax.dynamic_slice_in_dim(query_grads, spot * piece, piece, axis=2)
    smem = pl.BlockSpec(memory_space=pltpu.SMEM)
    vmem = pl.BlockSpec(memory_space=pltpu.VMEM)
    hbm = pl.BlockSpec(memory_space=pl.ANY)
    dma = pltpu.SemaphoreType.DMA
    return pl.pallas_call(
        functools.partial(kernel, nb, nx, names),
        out_shape=jax.ShapeDtypeStruct((rows, count), F32),
        in_specs=[smem, vmem, vmem, hbm, hbm, hbm],
        out_specs=vmem,
        scratch_shapes=[
            pltpu.VMEM((rows, blocks * piece), BF16),
            pltpu.VMEM(curvature.shape[1:], BF16),
            pltpu.VMEM((count, features), BF16),
            pltpu.VMEM((count, features), BF16),
            pltpu.VMEM((count, count), BF16),
            pltpu.VMEM((nb, rows, piece), BF16),
            pltpu.VMEM((queries, features), BF16),
            pltpu.VMEM((queries, features), BF16),
            pltpu.VMEM((rows, count), F32),
            pltpu.VMEM((nb, rows, count), BF16),
            pltpu.VMEM((nb, rows, count), BF16),
            dma((3,)),
            dma((nb,)),
            dma((nb,)),
            dma((nb, 2 * nx + 1)),
            dma((nb, 2 * nx + 1)),
            dma((nb, 2 * nx)),
            dma((nb, 2 * nx)),
            dma((nb,)),
            dma((nb,)),
        ],
        compiler_params=pltpu.CompilerParams(
            collective_id=0, has_side_effects=True, vmem_limit_bytes=62 * 2**20
        ),
        cost_estimate=pl.CostEstimate(
            flops=2 * queries * features * (curvature.shape[1] + count),
            bytes_accessed=8 * 2**20,
            transcendentals=0,
        ),
    )(
        block_map,
        query_ids.reshape(1, queries),
        row_ids,
        part.reshape(rows, blocks * piece),
        curvature.reshape(curvature.shape[1:]),
        train_grads.reshape(count, features),
    )


def solution(mesh):
    placed = (
        P("blk", None, "sub"),
        P("blk", ("row", "sub"), None),
        P(("parts", "row", "sub"), "blk", None),
        P("parts"),
        P(),
        P(("parts", "row", "sub")),
    )
    return jax.shard_map(
        functools.partial(per_device, mesh.shape["blk"], mesh.shape["row"], mesh.axis_names),
        mesh=mesh,
        in_specs=placed,
        out_specs=P("blk", ("parts", "row", "sub")),
        check_vma=False,
    )
```

```python
import functools

import jax
import jax.numpy as jnp
from jax import lax
from jax.experimental import pallas as pl
from jax.experimental.pallas import tpu as pltpu
from jax.sharding import PartitionSpec as P

MESH = pl.DeviceIdType.MESH
F32 = jnp.float32
BF16 = jnp.bfloat16
NT = (((1,), (1,)), ((), ()))


def aligned(index, size):
    return pl.ds(pl.multiple_of(index * size, size), size)


def kernel(
    nb, nx, names,
    block_map, query_ids, row_ids, q_hbm, curv_hbm, train_hbm, out_ref, last_ref,
    q_ref, curv, train, chosen, row_pick, stage, grouped, precond, mine, sent, arrived,
    load_sem, z_send, z_recv, a_send, a_recv, c_send, c_recv, e_send, e_recv,
):
    p, b, r, s = (lax.axis_index(name) for name in ("parts", "blk", "row", "sub"))
    rows = q_ref.shape[0]
    piece = q_ref.shape[1] // nb
    half = 2 * nx * piece
    own_cols = curv.shape[0]

    def at(parts=None, blk=None, row=None, sub=None):
        return (
            p if parts is None else parts,
            b if blk is None else blk,
            r if row is None else row,
            s if sub is None else sub,
        )

    loads = [
        pltpu.make_async_copy(q_hbm, q_ref, load_sem.at[0]),
        pltpu.make_async_copy(train_hbm, train, load_sem.at[1]),
        pltpu.make_async_copy(curv_hbm, curv, load_sem.at[2]),
    ]
    for load in loads:
        load.start()

    other = 1 - s
    mate = 1 - p
    peers = [lax.rem(r + o, nx) for o in range(nx)]
    origins = [lax.rem(r + nx - o, nx) for o in range(nx)]
    sources = [lax.rem(b + d, nb) for d in range(nb)]

    barrier = pltpu.get_barrier_semaphore()
    everyone = [at(blk=sources[d]) for d in range(1, nb)]
    everyone += [at(row=peers[o]) for o in range(1, nx)]
    everyone += [at(parts=mate), at(sub=other)]
    for device in everyone:
        pl.semaphore_signal(barrier, inc=1, device_id=device, device_id_type=MESH)

    loads[0].wait()
    for d in range(nb):
        target = lax.rem(b + nb - d, nb)

        def add(block, total, slot=block_map[target]):
            weight = jnp.where(slot == block, 1.0, 0.0)
            return total + weight * q_ref[:, aligned(block, piece)].astype(F32)

        zeros = jnp.zeros((rows, piece), F32)
        block = lax.fori_loop(0, nb, add, zeros, unroll=nb <= 8).astype(BF16)
        if d:
            stage[d] = block
        else:
            grouped[aligned(b, rows), aligned(s * 2 * nx + p * nx + r, piece)] = block
    pl.semaphore_wait(barrier, len(everyone))

    started = []

    def remote(ref_from, ref_to, send, recv, device):
        return pltpu.make_async_remote_copy(
            src_ref=ref_from, dst_ref=ref_to, send_sem=send, recv_sem=recv,
            device_id=device, device_id_type=MESH,
        )

    def go(*args):
        copy = remote(*args)
        copy.start()
        started.append(copy)

    def arrive(ref, send, recv):
        remote(ref, ref, send, recv, at(sub=other)).wait_recv()

    def spot(d, parts, row):
        return grouped.at[aligned(sources[d], rows), aligned(s * 2 * nx + parts * nx + row, piece)]

    def half_spot(d, sub):
        return grouped.at[aligned(sources[d], rows), aligned(sub, half)]

    def p_spot(e, row, sub):
        return precond.at[aligned(sources[e], rows), aligned(row * 2 + sub, own_cols)]

    for d in range(1, nb):
        go(stage.at[d], spot(0, p, r), z_send.at[d], z_recv.at[d], at(blk=lax.rem(b + nb - d, nb)))

    def spread(d):
        if d:
            arrive(spot(d, p, r), z_send.at[d], z_recv.at[d])
        for o in range(1, nx):
            go(spot(d, p, r), spot(d, p, r), a_send.at[d, o], a_recv.at[d, o], at(row=peers[o]))
        go(spot(d, p, r), spot(d, p, r), a_send.at[d, nx], a_recv.at[d, nx], at(parts=mate))

    def second(d):
        for o in range(1, nx):
            arrive(spot(d, p, origins[o]), a_send.at[d, o], a_recv.at[d, o])
            if d % 2 == 0:
                place = spot(d, p, origins[o])
                go(place, place, a_send.at[d, nx + o], a_recv.at[d, nx + o], at(parts=mate))
        arrive(spot(d, mate, r), a_send.at[d, nx], a_recv.at[d, nx])
        if d % 2 == 1:
            place = spot(d, mate, r)
            for o in range(1, nx):
                go(place, place, a_send.at[d, nx + o], a_recv.at[d, nx + o], at(row=peers[o]))

    def across(d):
        for o in range(1, nx):
            arrive(spot(d, mate, origins[o]), a_send.at[d, nx + o], a_recv.at[d, nx + o])
        place = half_spot(d, s)
        go(place, place, a_send.at[d, 2 * nx], a_recv.at[d, 2 * nx], at(sub=other))

    def settle(d):
        arrive(half_spot(d, other), a_send.at[d, 2 * nx], a_recv.at[d, 2 * nx])

    count = train.shape[0]
    width = train.shape[1] // nb

    def choose(d):
        if d == 0:
            loads[1].wait()
            pick = lax.broadcasted_iota(jnp.int32, (count, count), 0) == row_ids[...].reshape(1, count)
            row_pick[...] = jnp.where(pick, 1.0, 0.0).astype(BF16).T
        if width % 128 == 0 or d == 0:
            cols = pl.ds(d * width, width) if width % 128 == 0 else pl.ds(0, train.shape[1])
            chosen[:, cols] = jnp.dot(
                row_pick[...], train[:, cols], preferred_element_type=F32
            ).astype(BF16)

    def pipeline(steps, count):
        for t in range(count + max(lag for lag, _ in steps)):
            for lag, step in steps:
                if 0 <= t - lag < count:
                    step(t - lag)

    pipeline([(0, spread), (1, second), (0, choose), (2, across), (3, settle)], nb)
    loads[2].wait()

    def apply(e):
        outs = lax.broadcasted_iota(jnp.int32, (rows, grouped.shape[0]), 0) + sources[e] * rows
        pick = jnp.where(outs == query_ids[...], 1.0, 0.0).astype(BF16)
        ordered = jnp.dot(pick, grouped[...], preferred_element_type=F32).astype(BF16)
        result = lax.dot_general(ordered, curv[...], NT, preferred_element_type=F32)
        precond[aligned(sources[e], rows), aligned(r * 2 + s, own_cols)] = result.astype(BF16)
        place = p_spot(e, r, s)
        for o in range(1, nx):
            go(place, place, c_send.at[e, o], c_recv.at[e, o], at(row=peers[o]))
        go(place, place, c_send.at[e, 0], c_recv.at[e, 0], at(sub=other))

    def share(e):
        for o in range(1, nx):
            place = p_spot(e, origins[o], s)
            arrive(place, c_send.at[e, o], c_recv.at[e, o])
            go(place, place, c_send.at[e, nx + o], c_recv.at[e, nx + o], at(sub=other))

    def score(e):
        arrive(p_spot(e, r, other), c_send.at[e, 0], c_recv.at[e, 0])
        for o in range(1, nx):
            arrive(p_spot(e, origins[o], other), c_send.at[e, nx + o], c_recv.at[e, nx + o])
        result = lax.dot_general(
            precond[aligned(sources[e], rows), :], chosen[...], NT, preferred_element_type=F32
        )
        if e:
            sent[e] = result.astype(BF16)
            exchange(e).start()
        else:
            mine[...] = result

    def exchange(e):
        target = lax.rem(b + e, nb)
        return remote(sent.at[e], arrived.at[e], e_send.at[e], e_recv.at[e], at(blk=target))

    order = sorted(range(1, nb), key=lambda e: abs(2 * e - nb)) + [0]

    def turn(step):
        return lambda t: step(order[t])

    pipeline([(0, turn(apply)), (2, turn(score)), (1, turn(share))], nb)
    for copy in started:
        copy.wait_send()

    @pl.loop(1, nb - 1)
    def _(e):
        exchange(e).wait()
        mine[...] += arrived[e].astype(F32)

    out_ref[...] = mine[...]
    exchange(nb - 1).wait()
    last_ref[...] = arrived[nb - 1]


def per_device(nb, nx, names, query_grads, curvature, train_grads, query_ids, block_map, row_ids):
    rows, blocks, half = query_grads.shape
    queries = query_ids.shape[0]
    features = curvature.shape[2]
    count = train_grads.shape[0]
    piece = half // (2 * nx)
    spot = lax.axis_index("parts") * nx + lax.axis_index("row")
    part = lax.dynamic_slice_in_dim(query_grads, spot * piece, piece, axis=2)
    smem = pl.BlockSpec(memory_space=pltpu.SMEM)
    vmem = pl.BlockSpec(memory_space=pltpu.VMEM)
    hbm = pl.BlockSpec(memory_space=pl.ANY)
    dma = pltpu.SemaphoreType.DMA
    total, last = pl.pallas_call(
        functools.partial(kernel, nb, nx, names),
        out_shape=[jax.ShapeDtypeStruct((rows, count), kind) for kind in (F32, BF16)],
        in_specs=[smem, vmem, vmem, hbm, hbm, hbm],
        out_specs=[vmem, vmem],
        scratch_shapes=[
            pltpu.VMEM((rows, blocks * piece), BF16),
            pltpu.VMEM(curvature.shape[1:], BF16),
            pltpu.VMEM((count, features), BF16),
            pltpu.VMEM((count, features), BF16),
            pltpu.VMEM((count, count), BF16),
            pltpu.VMEM((nb, rows, piece), BF16),
            pltpu.VMEM((queries, features), BF16),
            pltpu.VMEM((queries, features), BF16),
            pltpu.VMEM((rows, count), F32),
            pltpu.VMEM((nb, rows, count), BF16),
            pltpu.VMEM((nb, rows, count), BF16),
            dma((3,)),
            dma((nb,)),
            dma((nb,)),
            dma((nb, 2 * nx + 1)),
            dma((nb, 2 * nx + 1)),
            dma((nb, 2 * nx)),
            dma((nb, 2 * nx)),
            dma((nb,)),
            dma((nb,)),
        ],
        compiler_params=pltpu.CompilerParams(
            collective_id=0, has_side_effects=True, vmem_limit_bytes=62 * 2**20
        ),
        cost_estimate=pl.CostEstimate(
            flops=2 * queries * features * (curvature.shape[1] + count),
            bytes_accessed=8 * 2**20,
            transcendentals=0,
        ),
    )(
        block_map,
        query_ids.reshape(1, queries),
        row_ids,
        part.reshape(rows, blocks * piece),
        curvature.reshape(curvature.shape[1:]),
        train_grads.reshape(count, features),
    )
    return total + last.astype(F32)


def solution(mesh):
    placed = (
        P("blk", None, "sub"),
        P("blk", ("row", "sub"), None),
        P(("parts", "row", "sub"), "blk", None),
        P("parts"),
        P(),
        P(("parts", "row", "sub")),
    )
    return jax.shard_map(
        functools.partial(per_device, mesh.shape["blk"], mesh.shape["row"], mesh.axis_names),
        mesh=mesh,
        in_specs=placed,
        out_specs=P("blk", ("parts", "row", "sub")),
        check_vma=False,
    )
```
